256 devices in a mesh: dp: 32 (over x, z), seq: 8 (over y, core).
Axes of the slice: x: 4, y: 4, z: 8, core: 2. Of those that a mesh axis runs over, the one named last changes fastest.
Arguments:
- queries: bfloat16 [32, 2048, 1536], P('dp', 'seq'), may hold values from -6 to 6
- keys: bfloat16 [32, 2048, 1536], P('dp', 'seq'), may hold values from -6 to 6
- values: bfloat16 [32, 2048, 1536], P('dp', 'seq'), may hold values from -6 to 6
- out_grad: bfloat16 [32, 2048, 1536], P('dp', 'seq'), may hold values from -6 to 6
- out_weight: bfloat16 [1536, 1536], P(None, 'dp'), may hold values from -0.15625 to 0.15625
- utterance: int32 [32, 2048], P('dp', 'seq'), may hold values from 0 to 7, never falling along the last dimension, each value on 1 to 1024 neighbouring positions
Outputs:
- query_grads: bfloat16 [32, 2048, 1536], P('dp', 'seq')
- key_grads: bfloat16 [32, 2048, 1536], P('dp', 'seq')
- value_grads: bfloat16 [32, 2048, 1536], P('dp', 'seq')
- projection_grad: float32 [1536, 1536], P('seq', 'dp')
The draws below stay inside these ranges and needn't reach their ends.
Inputs may be any that keep to these rules, and one draw needn't show every extreme that they name: In each pack the ids never fall along the frames; each utterance spans 1 to 1024 frames, and one spans exactly 1024.
All inputs are finite; a program needn't handle non-finite values.
Results may differ from the reference program's by a relative error of at most 0.03.
Values may be sent and summed in bfloat16 or wider, within the bound.
No kernel may reach another device: no remote copies, remote signals or barrier semaphores. Data moves between devices by JAX's collectives and lax.ppermute only.
A program may use at most 128 MiB of HBM per device.

```python
import math
import jax
import jax.numpy as jnp
import numpy as np
from jax import lax

D = 1536
HEADS = 16
UTTER = 8
FRAMES = 2048
MOST = 1024
PACKS = 32


def draw_queries(key, part):
    key = jax.random.fold_in(key, 3)
    return jax.random.truncated_normal(key, -6.0, 6.0, (PACKS, FRAMES, D), jnp.float32).astype(jnp.bfloat16)


def draw_keys(key, part):
    key = jax.random.fold_in(key, 5)
    return jax.random.truncated_normal(key, -6.0, 6.0, (PACKS, FRAMES, D), jnp.float32).astype(jnp.bfloat16)


def spiked(values, stream_key, source, target, blocks, factor):
    def block_of(dim):
        return (jnp.arange(values.shape[dim]) // (values.shape[dim] // blocks)).reshape((-1,) + (1,) * (values.ndim - 1 - dim))

    first = jax.random.permutation(stream_key, blocks)[block_of(target)]
    second = (block_of(target) + blocks // 2) % blocks
    return jnp.where((block_of(source) == first) | (block_of(source) == second), factor * values, values)


def levels(rng, dims, split, smallest, high):
    factor_of, own = 1.0, jax.random.fold_in(rng, 6)
    for dim, shards_of in split:
        heights = jnp.exp(jax.random.uniform(jax.random.fold_in(own, dim), (shards_of,), jnp.float32, smallest / len(split), high / len(split)))
        factor_of = factor_of * jnp.repeat(heights, dims[dim] // shards_of).reshape([-1 if axis == dim else 1 for axis in range(len(dims))])
    return factor_of


def profile(amount, total, reach, slope):
    portions = [(1 << 20) // math.isqrt(rank ** slope) + 1 for rank in range(2, amount + 1)]
    rest, counts = total - reach - (amount - 1), [1] * (amount - 1)
    while rest > 0:
        free = [i for i in range(amount - 1) if counts[i] < reach]
        pool, left = sum([portions[i] for i in free]), rest
        for i in free:
            extra = min(reach - counts[i], max(1, left * portions[i] // pool), rest)
            counts[i] = counts[i] + extra
            rest = rest - extra
    return np.array([reach] + counts)


def ragged_sizes(rng, number_of, total, reach, lean):
    if number_of == 2:
        one = jax.random.randint(rng, (), max(1, total - reach), min(reach, total - 1) + 1)
        return jnp.stack([one, total - one])
    sizes = jnp.asarray(profile(number_of, total, reach, lean), jnp.int32)
    pairs = (number_of - 1) // 2
    source_of, receiver = sizes[1:1 + 2 * pairs:2], sizes[2:2 + 2 * pairs:2]
    room = jnp.minimum(source_of - 1, reach - receiver)
    passed = jax.random.randint(jax.random.fold_in(rng, 1), (pairs,), 0, 1 << 20) % (room + 1)
    sizes = sizes.at[1:1 + 2 * pairs:2].set(source_of - passed).at[2:2 + 2 * pairs:2].set(receiver + passed)
    return sizes[jax.random.permutation(jax.random.fold_in(rng, 2), number_of)]


def normal_values(key, shape, width, most, shards=(), kind=jnp.bfloat16):
    values = jax.random.normal(key, shape, jnp.float32) * width
    if len(shards) > 0:
        values = levels(key, shape, shards, -0.22, 0.18) * values
    return jnp.clip(values, min=-most, max=most).astype(kind)


def gaussian_with(key, extent, deviation, reach, shards, heavy, held_as=jnp.bfloat16):
    values = deviation * jax.random.normal(key, extent, jnp.float32)
    if shards:
        values = values * levels(key, extent, shards, -0.22, 0.18)
    return jnp.clip(spiked(values, jax.random.fold_in(key, 3), *heavy), -reach, reach).astype(held_as)


def setup_inputs(seed: int = 0) -> dict:
    key_of = jax.random.split(jax.random.key(seed), 7)
    return {
        "queries": draw_queries(jax.random.fold_in(key_of[6], 71), 0),
        "keys": draw_keys(jax.random.fold_in(key_of[6], 71), 0),
        "values": normal_values(key_of[2], (PACKS, FRAMES, D), 1.0, 6.0, ((0, 32), (1, 8))),
        "out_grad": gaussian_with(key_of[3], (PACKS, FRAMES, D), 1.0, 6.0, ((0, 32), (1, 8)), (0, 2, 32, 2.75)),
        "out_weight": normal_values(key_of[4], (D, D), D ** -0.5, 0.15625, ((1, 32),)),
        "utterance": jax.vmap(lambda own: jnp.searchsorted(jnp.cumsum(ragged_sizes(own, UTTER, FRAMES, MOST, 2)), jnp.arange(FRAMES), side="right"))(jax.random.split(key_of[5], PACKS)).reshape((PACKS, FRAMES)).astype(jnp.int32),
    }


def head_backward(query_head, key_head, value_head, grad_head, same_utterance):
    scaling = 1.0 / math.sqrt(D // HEADS)
    scores = jnp.dot(query_head, key_head.T, preferred_element_type=jnp.float32) * scaling
    scores = jnp.where(same_utterance, scores, -1e+30)
    shifted = jnp.exp(scores - lax.optimization_barrier(jnp.max(scores, axis=1, keepdims=True)))
    weights = shifted / lax.optimization_barrier(jnp.sum(shifted, axis=1, keepdims=True))
    weights_low = weights.astype(jnp.bfloat16)
    context = jnp.dot(weights_low, value_head, preferred_element_type=jnp.float32).astype(jnp.bfloat16)
    weights_grad = jnp.dot(grad_head, value_head.T, preferred_element_type=jnp.float32)
    row_terms = lax.optimization_barrier(jnp.sum(grad_head.astype(jnp.float32) * context.astype(jnp.float32), axis=1, keepdims=True))
    score_grad = (weights * (weights_grad - row_terms) * scaling).astype(jnp.bfloat16)
    query_grad = jnp.dot(score_grad, key_head, preferred_element_type=jnp.float32).astype(jnp.bfloat16)
    key_grad = jnp.dot(score_grad.T, query_head, preferred_element_type=jnp.float32).astype(jnp.bfloat16)
    value_grad = jnp.dot(weights_low.T, grad_head, preferred_element_type=jnp.float32).astype(jnp.bfloat16)
    return (query_grad, key_grad, value_grad, context)

def split_heads(matrix):
    return matrix.reshape(FRAMES, HEADS, D // HEADS).transpose(1, 0, 2)

def join_heads(stacked):
    return stacked.transpose(1, 0, 2).reshape(FRAMES, D)

def reference(queries, keys, values, out_grad, out_weight, utterance):

    def one_pack(total, inputs):
        query_pack, key_pack, value_pack, grad_pack, pack_ids = inputs
        context_grad = jnp.dot(grad_pack, out_weight.T, preferred_element_type=jnp.float32).astype(jnp.bfloat16)
        same_utterance = pack_ids[:, None] == pack_ids[None, :]

        def per_head(group):
            return head_backward(group[0], group[1], group[2], group[3], same_utterance)
        results = lax.map(per_head, (split_heads(query_pack), split_heads(key_pack), split_heads(value_pack), split_heads(context_grad)))
        query_grad = join_heads(results[0])
        key_grad = join_heads(results[1])
        value_grad = join_heads(results[2])
        context = join_heads(results[3])
        total = total + jnp.dot(context.T, grad_pack, preferred_element_type=jnp.float32)
        return (total, (query_grad, key_grad, value_grad))
    start_total = jnp.zeros((D, D), jnp.float32)
    total, grads = lax.scan(one_pack, start_total, (queries, keys, values, out_grad, utterance))
    return (grads[0], grads[1], grads[2], total)
```

```python
import math

import jax
import jax.numpy as jnp
from jax import lax
from jax.experimental import pallas as pl
from jax.experimental.pallas import tpu as pltpu
from jax.sharding import PartitionSpec as P

D = 1536
HEADS = 16
HEAD = D // HEADS
SEQ = 8
OWN = HEADS // SEQ
WIDTH = OWN * HEAD
ROWS = 256
IDS = 16
SCALING = 1.0 / math.sqrt(HEAD)
LOG2E = math.log2(math.e)
EXCLUDED = -1e30
VMEM_BYTES = 56 * 1024 * 1024

BF16 = jnp.bfloat16
F32 = jnp.float32


def whole(count):
    return [pl.BlockSpec(memory_space=pltpu.VMEM)] * count


def dot(left, right, left_dim=1, right_dim=0):
    return lax.dot_general(
        left, right, (((left_dim,), (right_dim,)), ((), ())), preferred_element_type=F32
    )


def pack_kernel(query_ref, key_ref, value_ref, ids_ref, out_ref):
    for place, ref in enumerate((query_ref, key_ref, value_ref)):
        for tile in range(D // 128):
            turned = ref[0, :, tile * 128 : (tile + 1) * 128].T
            for half in range(2):
                row = tile * 128 + half * 64
                start = place * WIDTH + row % WIDTH
                out_ref[row // WIDTH, start : start + 64, :] = turned[half * 64 : half * 64 + 64]
    ids = jnp.broadcast_to(ids_ref[...].astype(F32), (IDS, ROWS)).astype(BF16)
    for block in range(SEQ):
        out_ref[block, 3 * WIDTH : 3 * WIDTH + IDS, :] = ids


def pack(queries, keys, values, utterance):
    return pl.pallas_call(
        pack_kernel,
        out_shape=jax.ShapeDtypeStruct((SEQ, 3 * WIDTH + IDS, ROWS), BF16),
        in_specs=whole(4),
        out_specs=pl.BlockSpec(memory_space=pltpu.VMEM),
        compiler_params=pltpu.CompilerParams(vmem_limit_bytes=VMEM_BYTES),
        cost_estimate=pl.CostEstimate(flops=10**7, bytes_accessed=5 * 10**6, transcendentals=0),
        name="pack",
    )(queries, keys, values, utterance)


def unpack_kernel(in_ref, query_ref, key_ref, value_ref):
    for place, ref in enumerate((query_ref, key_ref, value_ref)):
        for tile in range(D // 128):
            halves = []
            for half in range(2):
                row = tile * 128 + half * 64
                start = place * WIDTH + row % WIDTH
                halves.append(in_ref[row // WIDTH, start : start + 64, :])
            ref[0, :, tile * 128 : (tile + 1) * 128] = jnp.concatenate(halves, axis=0).T


def unpack(grads):
    shape = jax.ShapeDtypeStruct((1, ROWS, D), BF16)
    return pl.pallas_call(
        unpack_kernel,
        out_shape=(shape, shape, shape),
        in_specs=whole(1),
        out_specs=tuple(whole(3)),
        compiler_params=pltpu.CompilerParams(vmem_limit_bytes=VMEM_BYTES),
        cost_estimate=pl.CostEstimate(flops=10**7, bytes_accessed=5 * 10**6, transcendentals=0),
        name="unpack",
    )(grads)


def fold(tile, op):
    return op(tile.reshape(tile.shape[0] // 8, 8, tile.shape[1]), axis=0)


def rows_of(block):
    return pl.ds(pl.multiple_of(block * ROWS, ROWS), ROWS)


def key_ids(recv_ref, kid_ref):
    for block in range(SEQ):
        row = recv_ref[block, 3 * WIDTH : 3 * WIDTH + 1, :].astype(F32)
        kid_ref[block * ROWS : (block + 1) * ROWS, :] = jnp.broadcast_to(row, (128, ROWS)).T


def same(recv_ref, kid_ref, query_block, key_block):
    query_id = recv_ref[query_block, 3 * WIDTH : 3 * WIDTH + IDS, :].astype(F32)[0:1]
    key_id = kid_ref[rows_of(key_block), :]
    return jnp.concatenate([key_id, key_id], axis=1) == query_id


def forward_kernel(bounds_ref, recv_ref, context_ref, lse_ref, key_nat, kid_ref, score_ref):
    key_ids(recv_ref, kid_ref)
    for block in range(SEQ):
        for head in range(OWN):
            start = WIDTH + head * HEAD
            key_nat[head, block * ROWS : (block + 1) * ROWS, :] = recv_ref[
                block, start : start + HEAD, :
            ].T

    def query_block(index, _):
        low, high = bounds_ref[0, index], bounds_ref[1, index]
        queries = [
            recv_ref[index, head * HEAD : (head + 1) * HEAD, :] for head in range(OWN)
        ]

        def first(block, tops):
            keep = same(recv_ref, kid_ref, index, block)
            out = []
            for head in range(OWN):
                scores = dot(key_nat[head, rows_of(block), :], queries[head])
                scores = jnp.where(keep, scores, EXCLUDED)
                score_ref[head, block] = scores
                out.append(jnp.maximum(tops[head], fold(scores, jnp.max)))
            return tuple(out)

        tops = lax.fori_loop(
            low, high, first, tuple(jnp.full((8, ROWS), EXCLUDED, F32) for _ in range(OWN))
        )
        tops = [
            jnp.max(top, axis=0, keepdims=True) * (SCALING * LOG2E) for top in tops
        ]

        def second(block, carry):
            out = []
            for head in range(OWN):
                total, context = carry[head]
                start = 2 * WIDTH + head * HEAD
                shifted = jnp.exp2(score_ref[head, block] * (SCALING * LOG2E) - tops[head])
                total = total + fold(shifted, jnp.sum)
                context = context + dot(
                    recv_ref[block, start : start + HEAD, :], shifted.astype(BF16)
                )
                out.append((total, context))
            return tuple(out)

        done = lax.fori_loop(
            low,
            high,
            second,
            tuple(
                (jnp.zeros((8, ROWS), F32), jnp.zeros((HEAD, ROWS), F32)) for _ in range(OWN)
            ),
        )
        for head in range(OWN):
            total = jnp.sum(done[head][0], axis=0, keepdims=True)
            context_ref[index, head * HEAD : (head + 1) * HEAD, :] = (
                done[head][1] / total
            ).astype(BF16)
            lse_ref[index, head : head + 1, :] = tops[head] + jnp.log2(total)
        return 0

    lax.fori_loop(0, SEQ, query_block, 0)


def forward(bounds, recv):
    return pl.pallas_call(
        forward_kernel,
        out_shape=(
            jax.ShapeDtypeStruct((SEQ, WIDTH, ROWS), BF16),
            jax.ShapeDtypeStruct((SEQ, 8, ROWS), F32),
        ),
        in_specs=[pl.BlockSpec(memory_space=pltpu.SMEM)] + whole(1),
        out_specs=tuple(whole(2)),
        scratch_shapes=[
            pltpu.VMEM((OWN, SEQ * ROWS, HEAD), BF16),
            pltpu.VMEM((SEQ * ROWS, 128), F32),
            pltpu.VMEM((OWN, SEQ, ROWS, ROWS), F32),
        ],
        compiler_params=pltpu.CompilerParams(vmem_limit_bytes=VMEM_BYTES),
        cost_estimate=pl.CostEstimate(
            flops=4 * 10**9, bytes_accessed=4 * 10**6, transcendentals=8 * 10**6
        ),
        name="forward",
    )(bounds, recv)


PIECES = 10


def piece_rows(piece):
    return (0, 128) if piece in (6, 8) else (128, 128) if piece in (7, 9) else (0, 256)


def backward_kernel(*refs):
    bounds_ref, place_ref, recv_ref, context_ref, lse_ref, weight_ref = refs[:6]
    pieces = refs[6 : 6 + PIECES]
    out_ref = refs[6 + PIECES]
    (
        key_nat, value_nat, query_nat, grad_nat, grad_turned, row_ref, kid_ref, key_acc, value_acc,
    ) = refs[7 + PIECES :]
    key_ids(recv_ref, kid_ref)
    for block in range(SEQ):
        at = slice(block * ROWS, (block + 1) * ROWS)
        for head in range(OWN):
            for place, ref in enumerate((query_nat, key_nat, value_nat)):
                start = place * WIDTH + head * HEAD
                ref[head, at, :] = recv_ref[block, start : start + HEAD, :].T
            key_acc[head, at, :] = jnp.zeros((ROWS, HEAD), F32)
            value_acc[head, at, :] = jnp.zeros((ROWS, HEAD), F32)
    for number, piece in enumerate(pieces):
        block = place_ref[number]
        first, count = piece_rows(number)
        grads = dot(piece[...], weight_ref[...])
        low = grads.astype(BF16)
        turned = low.T
        at = pl.ds(pl.multiple_of(block * ROWS + first, 128), count)
        for head in range(OWN):
            grad_nat[head, at, :] = low[:, head * HEAD : (head + 1) * HEAD]
        grad_turned[block, :, first : first + count] = turned
    for block in range(SEQ):
        for head in range(OWN):
            at = slice(head * HEAD, (head + 1) * HEAD)
            row_ref[block, head : head + 1, :] = jnp.sum(
                grad_turned[block, at, :].astype(F32) * context_ref[block, at, :].astype(F32),
                axis=0,
                keepdims=True,
            )

    def query_block(index, _):
        low, high = bounds_ref[0, index], bounds_ref[1, index]
        at_query = rows_of(index)

        def key_block(block, totals):
            keep = same(recv_ref, kid_ref, index, block)
            at_key = rows_of(block)
            out = []
            for head in range(OWN):
                at = slice(head * HEAD, (head + 1) * HEAD)
                start = WIDTH + head * HEAD
                scores = dot(key_nat[head, at_key, :], recv_ref[index, at, :])
                scores = scores * (SCALING * LOG2E) - lse_ref[index, head : head + 1, :]
                weights = jnp.exp2(jnp.where(keep, scores, EXCLUDED))
                weights_low = weights.astype(BF16)
                weights_grad = dot(value_nat[head, at_key, :], grad_turned[index, at, :])
                score_grad = (weights * (weights_grad - row_ref[index, head : head + 1, :])).astype(BF16)
                value_acc[head, at_key, :] += dot(weights_low, grad_nat[head, at_query, :])
                key_acc[head, at_key, :] += dot(score_grad, query_nat[head, at_query, :])
                out.append(
                    totals[head] + dot(recv_ref[block, start : start + HEAD, :], score_grad)
                )
            return tuple(out)

        totals = lax.fori_loop(
            low, high, key_block, tuple(jnp.zeros((HEAD, ROWS), F32) for _ in range(OWN))
        )
        for head in range(OWN):
            out_ref[index, head * HEAD : (head + 1) * HEAD, :] = (totals[head] * SCALING).astype(
                BF16
            )
        return 0

    lax.fori_loop(0, SEQ, query_block, 0)
    for block in range(SEQ):
        at = slice(block * ROWS, (block + 1) * ROWS)
        for head in range(OWN):
            start = WIDTH + head * HEAD
            out_ref[block, start : start + HEAD, :] = (
                (key_acc[head, at, :] * SCALING).astype(BF16).T
            )
            start = 2 * WIDTH + head * HEAD
            out_ref[block, start : start + HEAD, :] = value_acc[head, at, :].astype(BF16).T


def backward(bounds, places, recv, context, lse, weight, pieces):
    natural = pltpu.VMEM((OWN, SEQ * ROWS, HEAD), BF16)
    total = pltpu.VMEM((OWN, SEQ * ROWS, HEAD), F32)
    return pl.pallas_call(
        backward_kernel,
        out_shape=jax.ShapeDtypeStruct((SEQ, 3 * WIDTH, ROWS), BF16),
        in_specs=[pl.BlockSpec(memory_space=pltpu.SMEM)] * 2 + whole(4 + PIECES),
        out_specs=pl.BlockSpec(memory_space=pltpu.VMEM),
        scratch_shapes=[
            natural,
            natural,
            natural,
            natural,
            pltpu.VMEM((SEQ, WIDTH, ROWS), BF16),
            pltpu.VMEM((SEQ, 8, ROWS), F32),
            pltpu.VMEM((SEQ * ROWS, 128), F32),
            total,
            total,
        ],
        compiler_params=pltpu.CompilerParams(vmem_limit_bytes=VMEM_BYTES),
        cost_estimate=pl.CostEstimate(
            flops=10**10, bytes_accessed=12 * 10**6, transcendentals=8 * 10**6
        ),
        name="backward",
    )(bounds, places, recv, context, lse, weight, *pieces)


def project_kernel(*refs):
    place_ref, context_ref = refs[:2]
    pieces = refs[2 : 2 + PIECES]
    out_ref, total_ref = refs[2 + PIECES :]
    for number, piece in enumerate(pieces):
        first, count = piece_rows(number)
        part = dot(context_ref[place_ref[number], :, first : first + count], piece[...])
        if number == 0:
            total_ref[...] = part
        else:
            total_ref[...] += part
    out_ref[...] = total_ref[...].astype(BF16).T


def project(places, context, pieces):
    return pl.pallas_call(
        project_kernel,
        out_shape=jax.ShapeDtypeStruct((D, WIDTH), BF16),
        in_specs=[pl.BlockSpec(memory_space=pltpu.SMEM)] + whole(1 + PIECES),
        out_specs=pl.BlockSpec(memory_space=pltpu.VMEM),
        scratch_shapes=[pltpu.VMEM((WIDTH, D), F32)],
        compiler_params=pltpu.CompilerParams(vmem_limit_bytes=VMEM_BYTES),
        cost_estimate=pl.CostEstimate(
            flops=12 * 10**8, bytes_accessed=7 * 10**6, transcendentals=0
        ),
        name="project",
    )(places, context, *pieces)


def along_y(step):
    return [(j, ((j // 2 + step) % 4) * 2 + j % 2) for j in range(SEQ)]


CORES = [(j, j ^ 1) for j in range(SEQ)]


def shards(queries, keys, values, out_grad, out_weight, utterance):
    packs = lax.axis_size("dp")
    me = lax.axis_index("seq")
    grads = out_grad[0]

    def send(array, pairs):
        return lax.ppermute(array, "seq", pairs)

    packed = pack(queries, keys, values, utterance)
    recv = lax.all_to_all(packed, "seq", split_axis=0, concat_axis=0)

    own_rows = lax.dynamic_slice_in_dim(out_weight, me * WIDTH, WIDTH, 0).T
    weight = lax.all_to_all(
        jnp.broadcast_to(own_rows[None], (packs,) + own_rows.shape), "dp", split_axis=0, concat_axis=0
    ).reshape(D, WIDTH)

    up, down = send(grads, along_y(1)), send(grads, along_y(3))
    far_up, far_down = send(up[:128], along_y(1)), send(down[128:], along_y(3))
    pieces = (
        grads, send(grads, CORES), up, send(up, CORES), down, send(down, CORES),
        far_up, far_down, send(far_up, CORES), send(far_down, CORES),
    )
    y, core = me // 2, me % 2

    def block_of(step, other):
        return ((y + step) % 4) * 2 + (core ^ other)

    places = jnp.stack(
        [
            block_of(0, 0), block_of(0, 1), block_of(3, 0), block_of(3, 1), block_of(1, 0),
            block_of(1, 1), block_of(2, 0), block_of(2, 0), block_of(2, 1), block_of(2, 1),
        ]
    ).astype(jnp.int32)

    ends = recv[:, 3 * WIDTH, :].astype(jnp.int32)
    first, last = ends[:, 0], ends[:, ROWS - 1]
    bounds = jnp.stack(
        [
            jnp.sum(last[None, :] < first[:, None], axis=1),
            jnp.sum(first[None, :] <= last[:, None], axis=1),
        ]
    ).astype(jnp.int32)

    context, lse = forward(bounds, recv)
    head_grads = backward(bounds, places, recv, context, lse, weight, pieces)
    received = lax.all_to_all(head_grads, "seq", split_axis=0, concat_axis=0)

    partial_rows = project(places, context, pieces).reshape(packs, D // packs, WIDTH)
    parts = lax.all_to_all(partial_rows, "dp", split_axis=0, concat_axis=0)
    projection_grad = jnp.sum(parts.astype(F32), axis=0).T

    query_grad, key_grad, value_grad = unpack(received)
    return (query_grad, key_grad, value_grad, projection_grad)


def solution(mesh):
    return jax.shard_map(
        shards,
        mesh=mesh,
        in_specs=(
            P("dp", "seq", None),
            P("dp", "seq", None),
            P("dp", "seq", None),
            P("dp", "seq", None),
            P(None, "dp"),
            P("dp", "seq"),
        ),
        out_specs=(
            P("dp", "seq", None),
            P("dp", "seq", None),
            P("dp", "seq", None),
            P("seq", "dp"),
        ),
        check_vma=False,
    )
```

```python
import functools
import math

import jax
import jax.numpy as jnp
from jax import lax
from jax.experimental import pallas as pl
from jax.experimental.pallas import tpu as pltpu
from jax.sharding import PartitionSpec as P

D = 1536
HEADS = 16
HEAD = D // HEADS
SEQ = 8
OWN = HEADS // SEQ
WIDTH = OWN * HEAD
ROWS = 256
IDS = 16
SCALING = 1.0 / math.sqrt(HEAD)
LOG2E = math.log2(math.e)
EXCLUDED = -1e30
VMEM_BYTES = 56 * 1024 * 1024

BF16 = jnp.bfloat16
F32 = jnp.float32


def whole(count):
    return [pl.BlockSpec(memory_space=pltpu.VMEM)] * count


def dot(left, right, left_dim=1, right_dim=0):
    return lax.dot_general(
        left, right, (((left_dim,), (right_dim,)), ((), ())), preferred_element_type=F32
    )


def pack_kernel(query_ref, key_ref, value_ref, ids_ref, *outs):
    for number, ref in enumerate((query_ref, key_ref, value_ref)):
        at = slice(number * HEAD, (number + 1) * HEAD)
        for group in range(SEQ // 2):
            width = 2 * WIDTH
            turned = ref[0, :, group * width : (group + 1) * width].T
            for part in range(2 * OWN):
                outs[part % OWN][2 * group + part // OWN, at, :] = turned[
                    part * HEAD : (part + 1) * HEAD
                ]
    ids = jnp.broadcast_to(ids_ref[...].astype(F32), (IDS, ROWS)).astype(BF16)
    for block in range(SEQ):
        outs[0][block, 3 * HEAD :, :] = ids


def pack(queries, keys, values, utterance):
    return pl.pallas_call(
        pack_kernel,
        out_shape=tuple(
            jax.ShapeDtypeStruct((SEQ, 3 * HEAD + (IDS if head == 0 else 0), ROWS), BF16)
            for head in range(OWN)
        ),
        in_specs=whole(4),
        out_specs=tuple(whole(OWN)),
        compiler_params=pltpu.CompilerParams(vmem_limit_bytes=VMEM_BYTES),
        cost_estimate=pl.CostEstimate(flops=2 * 10**10, bytes_accessed=5 * 10**6, transcendentals=0),
        name="pack",
    )(queries, keys, values, utterance)


def unpack_kernel(first_ref, second_ref, query_ref, key_ref, value_ref):
    for number, ref in enumerate((query_ref, key_ref, value_ref)):
        at = slice(number * HEAD, (number + 1) * HEAD)
        for group in range(SEQ // 2):
            parts = [
                part[block, at, :]
                for block in (2 * group, 2 * group + 1)
                for part in (first_ref, second_ref)
            ]
            width = 2 * WIDTH
            ref[0, :, group * width : (group + 1) * width] = jnp.concatenate(parts, axis=0).T


def unpack(first, second):
    shape = jax.ShapeDtypeStruct((1, ROWS, D), BF16)
    return pl.pallas_call(
        unpack_kernel,
        out_shape=(shape, shape, shape),
        in_specs=whole(2),
        out_specs=tuple(whole(3)),
        compiler_params=pltpu.CompilerParams(vmem_limit_bytes=VMEM_BYTES),
        cost_estimate=pl.CostEstimate(flops=10**7, bytes_accessed=5 * 10**6, transcendentals=0),
        name="unpack",
    )(first, second)


def fold(tile, op):
    return op(tile.reshape(tile.shape[0] // 8, 8, tile.shape[1]), axis=0)


def rows_of(block):
    return pl.ds(pl.multiple_of(block * ROWS, ROWS), ROWS)


NEAR = ((0, 256),) * 6
FAR = ((0, 128), (128, 128)) * 2


def gradient_kernel(rows, weight_ref, *refs):
    pieces, out_ref = refs[: len(rows)], refs[len(rows)]
    for number, (piece, (first, count)) in enumerate(zip(pieces, rows, strict=True)):
        local = sum(size for _, size in rows[:number]) // ROWS
        out_ref[local, :, first : first + count] = (
            dot(piece[...], weight_ref[...]).astype(BF16).T
        )


def gradients(weight, pieces, rows):
    blocks = sum(size for _, size in rows) // ROWS
    return pl.pallas_call(
        functools.partial(gradient_kernel, rows),
        out_shape=jax.ShapeDtypeStruct((blocks, WIDTH, ROWS), BF16),
        in_specs=whole(1 + len(rows)),
        out_specs=pl.BlockSpec(memory_space=pltpu.VMEM),
        compiler_params=pltpu.CompilerParams(vmem_limit_bytes=VMEM_BYTES),
        cost_estimate=pl.CostEstimate(
            flops=blocks * 16 * 10**7, bytes_accessed=blocks * 10**6, transcendentals=0
        ),
        name="gradients",
    )(weight, *pieces)


FIXED = 5
UNROLL = 4


def over(low, high, body, carry):
    if isinstance(high, list):
        return body(high, carry)
    chunk = UNROLL
    while chunk:
        steps = (high - low) // chunk
        carry = lax.fori_loop(
            0,
            steps,
            lambda step, held, low=low, chunk=chunk: body(
                [low + step * chunk + i for i in range(chunk)], held
            ),
            carry,
        )
        low = low + steps * chunk
        chunk //= 2
    return carry


def slot_of(block, high):
    return [other is block for other in high].index(True) if isinstance(high, list) else block


def each_block(place_ref, bounds_ref, query_block):
    def any_block(place, _):
        index = place_ref[place]
        low, high = bounds_ref[0, index], bounds_ref[1, index]
        for count in range(1, FIXED + 1):

            @pl.when(high - low == count)
            def _(count=count):
                query_block(place, low, [low + i for i in range(count)])

        @pl.when(high - low > FIXED)
        def _():
            query_block(place, low, high)

        return 0

    lax.fori_loop(0, SEQ, any_block, 0)


def attend_kernel(head, place_ref, bounds_ref, near_ref, far_ref, ids_ref, recv_ref, *refs):
    out_ref, context_ref, grads, kid_ref, key_nat, value_nat, score_ref, key_acc, value_acc = refs
    at = slice(head * HEAD, (head + 1) * HEAD)
    query_at, key_at, value_at = (slice(i * HEAD, (i + 1) * HEAD) for i in range(3))
    for block in range(SEQ):
        rows = slice(block * ROWS, (block + 1) * ROWS)
        key_nat[rows, :] = recv_ref[block, key_at, :].T
        value_nat[rows, :] = recv_ref[block, value_at, :].T
        kid_ref[rows, :] = jnp.broadcast_to(ids_ref[block, 0:1, :], (128, ROWS)).T
    grads[: len(NEAR)] = near_ref[:, at, :]
    grads[len(NEAR) :] = far_ref[:, at, :]
    key_acc[...] = jnp.zeros_like(key_acc)
    value_acc[...] = jnp.zeros_like(value_acc)

    def query_block(place, low, high):
        index = place_ref[place]
        queries = recv_ref[index, query_at, :]
        block_grads = grads[place]
        query_id = ids_ref[index, 0:1, :]

        def first(blocks, top):
            for block in blocks:
                key_id = kid_ref[rows_of(block), :]
                keep = jnp.concatenate([key_id, key_id], axis=1) == query_id
                scores = jnp.where(keep, dot(key_nat[rows_of(block), :], queries), EXCLUDED)
                score_ref[slot_of(block, high)] = scores
                top = jnp.maximum(top, fold(scores, jnp.max))
            return top

        top = over(low, high, first, jnp.full((8, ROWS), EXCLUDED, F32))
        top = jnp.max(top, axis=0, keepdims=True) * (SCALING * LOG2E)

        def second(blocks, carry):
            total, context = carry
            for block in blocks:
                shifted = jnp.exp2(score_ref[slot_of(block, high)] * (SCALING * LOG2E) - top)
                score_ref[slot_of(block, high)] = shifted
                total = total + fold(shifted, jnp.sum)
                context = context + dot(recv_ref[block, value_at, :], shifted.astype(BF16))
            return total, context

        total, context = over(
            low, high, second, (jnp.zeros((8, ROWS), F32), jnp.zeros((HEAD, ROWS), F32))
        )
        inverse = 1.0 / jnp.sum(total, axis=0, keepdims=True)
        context = (context * inverse).astype(BF16)
        context_ref[place] = context
        row_terms = jnp.sum(block_grads.astype(F32) * context.astype(F32), axis=0, keepdims=True)

        def third(blocks, query_total):
            added = []
            for block in blocks:
                rows = rows_of(block)
                weights = score_ref[slot_of(block, high)] * inverse
                weights_grad = dot(value_nat[rows, :], block_grads)
                score_grad = (weights * (weights_grad - row_terms)).astype(BF16)
                value_part = dot(weights.astype(BF16), block_grads, 1, 1)
                key_part = dot(score_grad, queries, 1, 1)
                query_total = query_total + dot(recv_ref[block, key_at, :], score_grad)
                added.append((rows, value_part, key_part))
            for rows, value_part, key_part in added:
                value_acc[rows, :] += value_part
                key_acc[rows, :] += key_part
            return query_total

        query_total = over(low, high, third, jnp.zeros((HEAD, ROWS), F32))
        out_ref[index, query_at, :] = (query_total * SCALING).astype(BF16)

    each_block(place_ref, bounds_ref, query_block)
    for block in range(SEQ):
        rows = slice(block * ROWS, (block + 1) * ROWS)
        out_ref[block, key_at, :] = (key_acc[rows, :] * SCALING).astype(BF16).T
        out_ref[block, value_at, :] = value_acc[rows, :].astype(BF16).T


def forward_kernel(head, place_ref, bounds_ref, ids_ref, recv_ref, *refs):
    context_ref, lse_ref, kid_ref, key_nat, score_ref = refs
    query_at, key_at, value_at = (slice(i * HEAD, (i + 1) * HEAD) for i in range(3))
    for block in range(SEQ):
        rows = slice(block * ROWS, (block + 1) * ROWS)
        key_nat[rows, :] = recv_ref[block, key_at, :].T
        kid_ref[rows, :] = jnp.broadcast_to(ids_ref[block, 0:1, :], (128, ROWS)).T

    def query_block(place, low, high):
        index = place_ref[place]
        queries = recv_ref[index, query_at, :]
        query_id = ids_ref[index, 0:1, :]

        def first(blocks, top):
            for block in blocks:
                key_id = kid_ref[rows_of(block), :]
                keep = jnp.concatenate([key_id, key_id], axis=1) == query_id
                scores = jnp.where(keep, dot(key_nat[rows_of(block), :], queries), EXCLUDED)
                score_ref[slot_of(block, high)] = scores
                top = jnp.maximum(top, fold(scores, jnp.max))
            return top

        top = over(low, high, first, jnp.full((8, ROWS), EXCLUDED, F32))
        top = jnp.max(top, axis=0, keepdims=True) * (SCALING * LOG2E)

        def second(blocks, carry):
            total, context = carry
            for block in blocks:
                shifted = jnp.exp2(score_ref[slot_of(block, high)] * (SCALING * LOG2E) - top)
                total = total + fold(shifted, jnp.sum)
                context = context + dot(recv_ref[block, value_at, :], shifted.astype(BF16))
            return total, context

        total, context = over(
            low, high, second, (jnp.zeros((8, ROWS), F32), jnp.zeros((HEAD, ROWS), F32))
        )
        total = jnp.sum(total, axis=0, keepdims=True)
        context_ref[place] = (context / total).astype(BF16)
        lse_ref[place] = jnp.broadcast_to(top + jnp.log2(total), (8, ROWS))

    each_block(place_ref, bounds_ref, query_block)


def forward(head, places, bounds, ids, recv):
    return pl.pallas_call(
        functools.partial(forward_kernel, head),
        out_shape=(
            jax.ShapeDtypeStruct((SEQ, HEAD, ROWS), BF16),
            jax.ShapeDtypeStruct((SEQ, 8, ROWS), F32),
        ),
        in_specs=[pl.BlockSpec(memory_space=pltpu.SMEM)] * 2 + whole(2),
        out_specs=tuple(whole(2)),
        scratch_shapes=[
            pltpu.VMEM((SEQ * ROWS, 128), F32),
            pltpu.VMEM((SEQ * ROWS, HEAD), BF16),
            pltpu.VMEM((SEQ, ROWS, ROWS), F32),
        ],
        compiler_params=pltpu.CompilerParams(vmem_limit_bytes=VMEM_BYTES),
        cost_estimate=pl.CostEstimate(
            flops=7 * 10**9, bytes_accessed=3 * 10**6, transcendentals=4 * 10**6
        ),
        name="forward",
    )(places, bounds, ids, recv)


def backward_kernel(
    head, place_ref, bounds_ref, near_ref, far_ref, ids_ref, recv_ref, context_ref, lse_ref, *refs
):
    out_ref, grads, kid_ref, key_nat, value_nat, key_acc, value_acc = refs
    at = slice(head * HEAD, (head + 1) * HEAD)
    query_at, key_at, value_at = (slice(i * HEAD, (i + 1) * HEAD) for i in range(3))
    for block in range(SEQ):
        rows = slice(block * ROWS, (block + 1) * ROWS)
        key_nat[rows, :] = recv_ref[block, key_at, :].T
        value_nat[rows, :] = recv_ref[block, value_at, :].T
        kid_ref[rows, :] = jnp.broadcast_to(ids_ref[block, 0:1, :], (128, ROWS)).T
    grads[: len(NEAR)] = near_ref[:, at, :]
    grads[len(NEAR) :] = far_ref[:, at, :]
    key_acc[...] = jnp.zeros_like(key_acc)
    value_acc[...] = jnp.zeros_like(value_acc)

    def query_block(place, low, high):
        index = place_ref[place]
        queries = recv_ref[index, query_at, :]
        query_id = ids_ref[index, 0:1, :]
        block_grads = grads[place]
        lse = lse_ref[place, 0:1, :]
        row_terms = jnp.sum(
            block_grads.astype(F32) * context_ref[place].astype(F32), axis=0, keepdims=True
        )

        def third(blocks, query_total):
            added = []
            for block in blocks:
                rows = rows_of(block)
                key_id = kid_ref[rows, :]
                keep = jnp.concatenate([key_id, key_id], axis=1) == query_id
                scores = dot(key_nat[rows, :], queries) * (SCALING * LOG2E) - lse
                weights = jnp.exp2(jnp.where(keep, scores, EXCLUDED))
                weights_grad = dot(value_nat[rows, :], block_grads)
                score_grad = (weights * (weights_grad - row_terms)).astype(BF16)
                value_part = dot(weights.astype(BF16), block_grads, 1, 1)
                key_part = dot(score_grad, queries, 1, 1)
                query_total = query_total + dot(recv_ref[block, key_at, :], score_grad)
                added.append((rows, value_part, key_part))
            for rows, value_part, key_part in added:
                value_acc[rows, :] += value_part
                key_acc[rows, :] += key_part
            return query_total

        query_total = over(low, high, third, jnp.zeros((HEAD, ROWS), F32))
        out_ref[index, query_at, :] = (query_total * SCALING).astype(BF16)

    each_block(place_ref, bounds_ref, query_block)
    for block in range(SEQ):
        rows = slice(block * ROWS, (block + 1) * ROWS)
        out_ref[block, key_at, :] = (key_acc[rows, :] * SCALING).astype(BF16).T
        out_ref[block, value_at, :] = value_acc[rows, :].astype(BF16).T


def backward(head, places, bounds, near, far, ids, recv, context, lse):
    return pl.pallas_call(
        functools.partial(backward_kernel, head),
        out_shape=jax.ShapeDtypeStruct((SEQ, 3 * HEAD, ROWS), BF16),
        in_specs=[pl.BlockSpec(memory_space=pltpu.SMEM)] * 2 + whole(6),
        out_specs=pl.BlockSpec(memory_space=pltpu.VMEM),
        scratch_shapes=[
            pltpu.VMEM((SEQ, HEAD, ROWS), BF16),
            pltpu.VMEM((SEQ * ROWS, 128), F32),
            pltpu.VMEM((SEQ * ROWS, HEAD), BF16),
            pltpu.VMEM((SEQ * ROWS, HEAD), BF16),
            pltpu.VMEM((SEQ * ROWS, HEAD), F32),
            pltpu.VMEM((SEQ * ROWS, HEAD), F32),
        ],
        compiler_params=pltpu.CompilerParams(vmem_limit_bytes=VMEM_BYTES),
        cost_estimate=pl.CostEstimate(
            flops=15 * 10**9, bytes_accessed=6 * 10**6, transcendentals=4 * 10**6
        ),
        name="backward",
    )(places, bounds, near, far, ids, recv, context, lse)


def attend(head, places, bounds, near, far, ids, recv):
    return pl.pallas_call(
        functools.partial(attend_kernel, head),
        out_shape=(
            jax.ShapeDtypeStruct((SEQ, 3 * HEAD, ROWS), BF16),
            jax.ShapeDtypeStruct((SEQ, HEAD, ROWS), BF16),
        ),
        in_specs=[pl.BlockSpec(memory_space=pltpu.SMEM)] * 2 + whole(4),
        out_specs=tuple(whole(2)),
        scratch_shapes=[
            pltpu.VMEM((SEQ, HEAD, ROWS), BF16),
            pltpu.VMEM((SEQ * ROWS, 128), F32),
            pltpu.VMEM((SEQ * ROWS, HEAD), BF16),
            pltpu.VMEM((SEQ * ROWS, HEAD), BF16),
            pltpu.VMEM((SEQ, ROWS, ROWS), F32),
            pltpu.VMEM((SEQ * ROWS, HEAD), F32),
            pltpu.VMEM((SEQ * ROWS, HEAD), F32),
        ],
        compiler_params=pltpu.CompilerParams(vmem_limit_bytes=VMEM_BYTES),
        cost_estimate=pl.CostEstimate(
            flops=2 * 10**10, bytes_accessed=6 * 10**6, transcendentals=4 * 10**6
        ),
        name="attend",
    )(places, bounds, near, far, ids, recv)


def folded(part):
    half = part.shape[0] // 2
    return jnp.concatenate(
        [part[:, :128], jnp.concatenate([part[:half, 128:], part[half:, 128:]], axis=1)], axis=0
    )


def unfolded(part):
    columns = part.shape[0] * 2 // 3
    right = jnp.concatenate([part[columns:, :64], part[columns:, 64:]], axis=0)
    return jnp.concatenate([part[:columns], right], axis=1)


def project_kernel(columns, *refs):
    rows = NEAR + FAR
    contexts, pieces, (out_ref, total_ref) = refs[:OWN], refs[OWN:-2], refs[-2:]
    for number, (piece, (first, count)) in enumerate(zip(pieces, rows, strict=True)):
        local = sum(size for _, size in rows[:number]) // ROWS
        for head, context_ref in enumerate(contexts):
            at = slice(head * HEAD, (head + 1) * HEAD)
            part = dot(context_ref[local, :, first : first + count], piece[...])
            if number == 0:
                total_ref[at, :] = part
            else:
                total_ref[at, :] += part
    turned = total_ref[...].T
    for owner in range(D // columns):
        part = turned[owner * columns : (owner + 1) * columns]
        out_ref[owner] = folded(part).astype(BF16)


def project(columns, contexts, pieces):
    return pl.pallas_call(
        functools.partial(project_kernel, columns),
        out_shape=jax.ShapeDtypeStruct((D // columns, columns * 3 // 2, 128), BF16),
        in_specs=whole(OWN + len(pieces)),
        out_specs=pl.BlockSpec(memory_space=pltpu.VMEM),
        scratch_shapes=[pltpu.VMEM((WIDTH, D), F32)],
        compiler_params=pltpu.CompilerParams(vmem_limit_bytes=VMEM_BYTES),
        cost_estimate=pl.CostEstimate(
            flops=12 * 10**8, bytes_accessed=7 * 10**6, transcendentals=0
        ),
        name="project",
    )(*contexts, *pieces)


PLACES = ((0, 0), (0, 1), (3, 0), (3, 1), (1, 0), (1, 1), (2, 0), (2, 1))


def moved(j, step, other):
    return ((j // 2 + step) % 4) * 2 + (j % 2 ^ other)


def after(arrays, *others):
    return lax.optimization_barrier((arrays, others))[0]


def shards(queries, keys, values, out_grad, out_weight, utterance):
    packs = lax.axis_size("dp")
    me = lax.axis_index("seq")
    grads = out_grad[0]
    places = jnp.stack([moved(me, *place) for place in PLACES]).astype(jnp.int32)

    def send(array, step, other):
        return lax.ppermute(array, "seq", [(j, moved(j, step, other)) for j in range(SEQ)])

    def swap(array):
        return lax.all_to_all(array, "seq", split_axis=0, concat_axis=0)

    up, down = send(grads, 1, 0), send(grads, 3, 0)
    swapped = send(grads, 0, 1)
    far_up, far_down = send(up[:128], 1, 0), send(down[128:], 3, 0)
    near = (grads, swapped, up, send(up, 0, 1), down, send(down, 0, 1))

    packed = pack(queries, keys, values, utterance)
    own_rows = lax.dynamic_slice_in_dim(out_weight, me * WIDTH, WIDTH, 0).T
    own_rows = folded(own_rows)
    own_rows = jnp.broadcast_to(own_rows[None], (packs,) + own_rows.shape)
    weight = lax.all_to_all(own_rows, "dp", split_axis=0, concat_axis=0)
    weight = jax.vmap(unfolded)(weight).reshape(D, WIDTH)

    first_recv = swap(after(packed[0], weight, far_up, far_down))
    second_recv = swap(after(packed[1], first_recv))
    near_grads = gradients(weight, near, NEAR)
    far_up, far_down = after((far_up, far_down), near_grads)
    far = (far_up, far_down, send(far_up, 0, 1), send(far_down, 0, 1))
    far_grads = gradients(weight, far, FAR)

    ids = first_recv[:, 3 * HEAD : 3 * HEAD + 8, :].astype(F32)
    starts, ends = ids[:, 0, 0], ids[:, 0, ROWS - 1]
    bounds = jnp.stack(
        [
            jnp.sum(ends[None, :] < starts[:, None], axis=1),
            jnp.sum(starts[None, :] <= ends[:, None], axis=1),
        ]
    ).astype(jnp.int32)

    first_grads, first_context = attend(
        0, places, bounds, near_grads, far_grads, ids, first_recv
    )
    first_out = swap(after(first_grads, second_recv))
    second_context, lse = forward(
        1, places, after(bounds, first_grads), after(ids, second_recv), second_recv
    )

    own_part = project(D // packs, (first_context, second_context), near + far)
    parts = lax.all_to_all(after(own_part, first_out), "dp", split_axis=0, concat_axis=0)
    projection_grad = unfolded(jnp.sum(parts.astype(F32), axis=0)).T

    second_grads = backward(
        1, places, bounds, near_grads, far_grads, ids, second_recv, second_context, lse
    )
    second_out = swap(after(second_grads, parts))
    query_grad, key_grad, value_grad = unpack(first_out, second_out)
    return (query_grad, key_grad, value_grad, projection_grad)


def solution(mesh):
    return jax.shard_map(
        shards,
        mesh=mesh,
        in_specs=(
            P("dp", "seq", None),
            P("dp", "seq", None),
            P("dp", "seq", None),
            P("dp", "seq", None),
            P(None, "dp"),
            P("dp", "seq"),
        ),
        out_specs=(
            P("dp", "seq", None),
            P("dp", "seq", None),
            P("dp", "seq", None),
            P("seq", "dp"),
        ),
        check_vma=False,
    )
```

```python
import functools
import math

import jax
import jax.numpy as jnp
from jax import lax
from jax.experimental import pallas as pl
from jax.experimental.pallas import tpu as pltpu
from jax.sharding import PartitionSpec as P

D = 1536
HEADS = 16
HEAD = D // HEADS
SEQ = 8
OWN = HEADS // SEQ
WIDTH = OWN * HEAD
ROWS = 256
IDS = 16
SCALING = 1.0 / math.sqrt(HEAD)
LOG2E = math.log2(math.e)
EXCLUDED = -1e30
VMEM_BYTES = 20 * 1024 * 1024
ATTENTION_VMEM_BYTES = 56 * 1024 * 1024

BF16 = jnp.bfloat16
F32 = jnp.float32


def whole(count):
    return [pl.BlockSpec(memory_space=pltpu.VMEM)] * count


def dot(left, right, left_dim=1, right_dim=0):
    return lax.dot_general(
        left, right, (((left_dim,), (right_dim,)), ((), ())), preferred_element_type=F32
    )


def pack_kernel(query_ref, key_ref, value_ref, ids_ref, *outs):
    for number, ref in enumerate((query_ref, key_ref, value_ref)):
        at = slice(number * HEAD, (number + 1) * HEAD)
        for group in range(SEQ // 2):
            width = 2 * WIDTH
            turned = ref[0, :, group * width : (group + 1) * width].T
            for part in range(2 * OWN):
                outs[part % OWN][2 * group + part // OWN, at, :] = turned[
                    part * HEAD : (part + 1) * HEAD
                ]
    ids = jnp.broadcast_to(ids_ref[...].astype(F32), (IDS, ROWS)).astype(BF16)
    for block in range(SEQ):
        outs[0][block, 3 * HEAD :, :] = ids


def pack(queries, keys, values, utterance):
    return pl.pallas_call(
        pack_kernel,
        out_shape=tuple(
            jax.ShapeDtypeStruct((SEQ, 3 * HEAD + (IDS if head == 0 else 0), ROWS), BF16)
            for head in range(OWN)
        ),
        in_specs=whole(4),
        out_specs=tuple(whole(OWN)),
        compiler_params=pltpu.CompilerParams(vmem_limit_bytes=VMEM_BYTES),
        cost_estimate=pl.CostEstimate(flops=2 * 10**10, bytes_accessed=5 * 10**6, transcendentals=0),
        name="pack",
    )(queries, keys, values, utterance)


def unpack_kernel(first_ref, second_ref, query_ref, key_ref, value_ref):
    for number, ref in enumerate((query_ref, key_ref, value_ref)):
        at = slice(number * HEAD, (number + 1) * HEAD)
        for group in range(SEQ // 2):
            parts = [
                part[block, at, :]
                for block in (2 * group, 2 * group + 1)
                for part in (first_ref, second_ref)
            ]
            width = 2 * WIDTH
            ref[0, :, group * width : (group + 1) * width] = jnp.concatenate(parts, axis=0).T


def unpack(first, second):
    steps = 2
    rows = ROWS // steps
    shape = jax.ShapeDtypeStruct((1, ROWS, D), BF16)
    part = pl.BlockSpec((SEQ, 3 * HEAD, rows), lambda step: (0, 0, step))
    whole_rows = pl.BlockSpec((1, rows, D), lambda step: (0, step, 0))
    return pl.pallas_call(
        unpack_kernel,
        grid=(steps,),
        out_shape=(shape, shape, shape),
        in_specs=[part, part],
        out_specs=(whole_rows,) * 3,
        compiler_params=pltpu.CompilerParams(vmem_limit_bytes=VMEM_BYTES),
        cost_estimate=pl.CostEstimate(flops=10**7, bytes_accessed=5 * 10**6, transcendentals=0),
        name="unpack",
    )(first, second)


def fold(tile, op):
    return op(tile.reshape(tile.shape[0] // 8, 8, tile.shape[1]), axis=0)


def rows_of(block):
    return pl.ds(pl.multiple_of(block * ROWS, ROWS), ROWS)


NEAR = ((0, 256),) * 6
FAR = ((0, 128), (128, 128)) * 2


def gradient_kernel(rows, weight_ref, *refs):
    pieces, out_ref = refs[: len(rows)], refs[len(rows)]
    for number, (piece, (first, count)) in enumerate(zip(pieces, rows, strict=True)):
        local = sum(size for _, size in rows[:number]) // ROWS
        out_ref[local, :, first : first + count] = (
            dot(piece[...], weight_ref[...]).astype(BF16).T
        )


def gradients(weight, pieces, rows):
    blocks = sum(size for _, size in rows) // ROWS
    return pl.pallas_call(
        functools.partial(gradient_kernel, rows),
        out_shape=jax.ShapeDtypeStruct((blocks, WIDTH, ROWS), BF16),
        in_specs=whole(1 + len(rows)),
        out_specs=pl.BlockSpec(memory_space=pltpu.VMEM),
        compiler_params=pltpu.CompilerParams(vmem_limit_bytes=VMEM_BYTES),
        cost_estimate=pl.CostEstimate(
            flops=blocks * 16 * 10**7, bytes_accessed=blocks * 10**6, transcendentals=0
        ),
        name="gradients",
    )(weight, *pieces)


FIXED = 5
UNROLL = 4


def over(low, high, body, carry):
    if isinstance(high, list):
        return body(high, carry)
    chunk = UNROLL
    while chunk:
        steps = (high - low) // chunk
        carry = lax.fori_loop(
            0,
            steps,
            lambda step, held, low=low, chunk=chunk: body(
                [low + step * chunk + i for i in range(chunk)], held
            ),
            carry,
        )
        low = low + steps * chunk
        chunk //= 2
    return carry


def slot_of(block, high):
    return [other is block for other in high].index(True) if isinstance(high, list) else block


def each_block(place_ref, bounds_ref, query_block):
    def any_block(place, _):
        index = place_ref[place]
        low, high = bounds_ref[0, index], bounds_ref[1, index]
        for count in range(1, FIXED + 1):

            @pl.when(high - low == count)
            def _(count=count):
                query_block(place, low, [low + i for i in range(count)])

        @pl.when(high - low > FIXED)
        def _():
            query_block(place, low, high)

        return 0

    lax.fori_loop(0, SEQ, any_block, 0)


def attend_kernel(head, place_ref, bounds_ref, near_ref, far_ref, recv_ref, *refs):
    if head == 0:
        out_ref, context_ref, ids_ref, *refs = refs
    else:
        ids_ref, out_ref, context_ref, *refs = refs
    grads, kid_ref, key_nat, value_nat, score_ref, key_acc, value_acc = refs
    at = slice(head * HEAD, (head + 1) * HEAD)
    query_at, key_at, value_at = (slice(i * HEAD, (i + 1) * HEAD) for i in range(3))
    for block in range(SEQ):
        rows = slice(block * ROWS, (block + 1) * ROWS)
        key_nat[rows, :] = recv_ref[block, key_at, :].T
        value_nat[rows, :] = recv_ref[block, value_at, :].T
        if head == 0:
            ids_ref[block] = recv_ref[block, 3 * HEAD :, :].astype(F32)[:8]
        kid_ref[rows, :] = jnp.broadcast_to(ids_ref[block, 0:1, :], (128, ROWS)).T
    grads[: len(NEAR)] = near_ref[:, at, :]
    grads[len(NEAR) :] = far_ref[:, at, :]
    key_acc[...] = jnp.zeros_like(key_acc)
    value_acc[...] = jnp.zeros_like(value_acc)

    def query_block(place, low, high):
        index = place_ref[place]
        queries = recv_ref[index, query_at, :]
        block_grads = grads[place]
        query_id = ids_ref[index, 0:1, :]

        def first(blocks, top):
            for block in blocks:
                key_id = kid_ref[rows_of(block), :]
                keep = jnp.concatenate([key_id, key_id], axis=1) == query_id
                scores = jnp.where(keep, dot(key_nat[rows_of(block), :], queries), EXCLUDED)
                score_ref[slot_of(block, high)] = scores
                top = jnp.maximum(top, fold(scores, jnp.max))
            return top

        top = over(low, high, first, jnp.full((8, ROWS), EXCLUDED, F32))
        top = jnp.max(top, axis=0, keepdims=True) * (SCALING * LOG2E)

        def second(blocks, carry):
            total, context = carry
            for block in blocks:
                shifted = jnp.exp2(score_ref[slot_of(block, high)] * (SCALING * LOG2E) - top)
                score_ref[slot_of(block, high)] = shifted
                total = total + fold(shifted, jnp.sum)
                context = context + dot(recv_ref[block, value_at, :], shifted.astype(BF16))
            return total, context

        total, context = over(
            low, high, second, (jnp.zeros((8, ROWS), F32), jnp.zeros((HEAD, ROWS), F32))
        )
        inverse = 1.0 / jnp.sum(total, axis=0, keepdims=True)
        context = (context * inverse).astype(BF16)
        context_ref[place] = context
        row_terms = jnp.sum(block_grads.astype(F32) * context.astype(F32), axis=0, keepdims=True)

        def third(blocks, query_total):
            added = []
            for block in blocks:
                rows = rows_of(block)
                weights = score_ref[slot_of(block, high)] * inverse
                weights_grad = dot(value_nat[rows, :], block_grads)
                score_grad = (weights * (weights_grad - row_terms)).astype(BF16)
                value_part = dot(weights.astype(BF16), block_grads, 1, 1)
                key_part = dot(score_grad, queries, 1, 1)
                query_total = query_total + dot(recv_ref[block, key_at, :], score_grad)
                added.append((rows, value_part, key_part))
            for rows, value_part, key_part in added:
                value_acc[rows, :] += value_part
                key_acc[rows, :] += key_part
            return query_total

        query_total = over(low, high, third, jnp.zeros((HEAD, ROWS), F32))
        out_ref[index, query_at, :] = (query_total * SCALING).astype(BF16)

    each_block(place_ref, bounds_ref, query_block)
    for block in range(SEQ):
        rows = slice(block * ROWS, (block + 1) * ROWS)
        out_ref[block, key_at, :] = (key_acc[rows, :] * SCALING).astype(BF16).T
        out_ref[block, value_at, :] = value_acc[rows, :].astype(BF16).T


def attend(head, places, bounds, near, far, recv, ids=()):
    shapes = [
        jax.ShapeDtypeStruct((SEQ, 3 * HEAD, ROWS), BF16),
        jax.ShapeDtypeStruct((SEQ, HEAD, ROWS), BF16),
    ]
    if head == 0:
        shapes.append(jax.ShapeDtypeStruct((SEQ, 8, ROWS), F32))
    return pl.pallas_call(
        functools.partial(attend_kernel, head),
        out_shape=tuple(shapes),
        in_specs=[pl.BlockSpec(memory_space=pltpu.SMEM)] * 2 + whole(3 + len(ids)),
        out_specs=tuple(whole(len(shapes))),
        scratch_shapes=[
            pltpu.VMEM((SEQ, HEAD, ROWS), BF16),
            pltpu.VMEM((SEQ * ROWS, 128), F32),
            pltpu.VMEM((SEQ * ROWS, HEAD), BF16),
            pltpu.VMEM((SEQ * ROWS, HEAD), BF16),
            pltpu.VMEM((SEQ, ROWS, ROWS), F32),
            pltpu.VMEM((SEQ * ROWS, HEAD), F32),
            pltpu.VMEM((SEQ * ROWS, HEAD), F32),
        ],
        compiler_params=pltpu.CompilerParams(vmem_limit_bytes=ATTENTION_VMEM_BYTES),
        cost_estimate=pl.CostEstimate(
            flops=2 * 10**10, bytes_accessed=6 * 10**6, transcendentals=4 * 10**6
        ),
        name="attend",
    )(places, bounds, near, far, recv, *ids)


def folded(part):
    half = part.shape[0] // 2
    return jnp.concatenate(
        [part[:, :128], jnp.concatenate([part[:half, 128:], part[half:, 128:]], axis=1)], axis=0
    )


def unfolded(part):
    columns = part.shape[0] * 2 // 3
    right = jnp.concatenate([part[columns:, :64], part[columns:, 64:]], axis=0)
    return jnp.concatenate([part[:columns], right], axis=1)


def project_kernel(columns, depth, x_ref, *refs):
    rows = NEAR + FAR
    contexts, refs = refs[:OWN], refs[OWN:]
    pieces, outs, (total_ref, turned_ref) = refs[: len(rows)], refs[len(rows) : -2], refs[-2:]
    for number, (piece, (first, count)) in enumerate(zip(pieces, rows, strict=True)):
        local = sum(size for _, size in rows[:number]) // ROWS
        context = jnp.concatenate([ref[local, :, first : first + count] for ref in contexts], axis=0)
        part = dot(context, piece[...])
        if number == 0:
            total_ref[...] = part
        else:
            total_ref[...] += part
    turned_ref[...] = total_ref[...].T
    for step, out_ref in enumerate(outs):
        for z in range(depth):
            start = pl.multiple_of((x_ref[step] * depth + z) * columns, 16)
            out_ref[z] = folded(turned_ref[pl.ds(start, columns), :]).astype(BF16)


def project(columns, depth, order, contexts, pieces):
    across = order.shape[0]
    return pl.pallas_call(
        functools.partial(project_kernel, columns, depth),
        out_shape=(jax.ShapeDtypeStruct((depth, columns * 3 // 2, 128), BF16),) * across,
        in_specs=[pl.BlockSpec(memory_space=pltpu.SMEM)] + whole(OWN + len(pieces)),
        out_specs=tuple(whole(across)),
        scratch_shapes=[pltpu.VMEM((WIDTH, D), F32), pltpu.VMEM((D, WIDTH), F32)],
        compiler_params=pltpu.CompilerParams(vmem_limit_bytes=VMEM_BYTES),
        cost_estimate=pl.CostEstimate(
            flops=12 * 10**8, bytes_accessed=7 * 10**6, transcendentals=0
        ),
        name="project",
    )(order, *contexts, *pieces)


PLACES = ((0, 0), (0, 1), (3, 0), (3, 1), (1, 0), (1, 1), (2, 0), (2, 1))


def moved(j, step, other):
    return ((j // 2 + step) % 4) * 2 + (j % 2 ^ other)


def after(arrays, *others):
    return lax.optimization_barrier((arrays, others))[0]


def shards(queries, keys, values, out_grad, out_weight, utterance):
    packs = lax.axis_size("dp")
    depth = math.gcd(packs, 8)
    me, position = lax.axis_index("seq"), lax.axis_index("dp")
    grads = out_grad[0]
    places = jnp.stack([moved(me, *place) for place in PLACES]).astype(jnp.int32)

    def send(array, step, other):
        return lax.ppermute(array, "seq", [(j, moved(j, step, other)) for j in range(SEQ)])

    def swap(array):
        return lax.all_to_all(array, "seq", split_axis=0, concat_axis=0)

    up, down = send(grads, 1, 0), send(grads, 3, 0)
    swapped = send(grads, 0, 1)
    far_up, far_down = send(up[:128], 1, 0), send(down[128:], 3, 0)
    near = (grads, swapped, up, send(up, 0, 1), down, send(down, 0, 1))

    packed = pack(queries, keys, values, utterance)
    own_rows = lax.dynamic_slice_in_dim(out_weight, me * WIDTH, WIDTH, 0).T
    own_rows = folded(own_rows)
    own_rows = jnp.broadcast_to(own_rows[None], (packs,) + own_rows.shape)
    folded_weight = lax.all_to_all(own_rows, "dp", split_axis=0, concat_axis=0)
    weight = jax.vmap(unfolded)(folded_weight).reshape(D, WIDTH)

    first_recv = swap(after(packed[0], folded_weight, far_up, far_down))
    second_recv = swap(after(packed[1], first_recv))
    near_grads = gradients(weight, near, NEAR)
    far_up, far_down = after((far_up, far_down), near_grads)
    far = (far_up, far_down, send(far_up, 0, 1), send(far_down, 0, 1))
    far_grads = gradients(weight, far, FAR)

    starts, ends = (first_recv[:, 3 * HEAD, at].astype(jnp.int32) for at in (0, ROWS - 1))
    bounds = jnp.stack(
        [
            jnp.sum(ends[None, :] < starts[:, None], axis=1),
            jnp.sum(starts[None, :] <= ends[:, None], axis=1),
        ]
    ).astype(jnp.int32)

    first_grads, first_context, ids = attend(
        0, places, bounds, near_grads, far_grads, first_recv
    )
    first_out = swap(after(first_grads, second_recv))
    second_grads, second_context = attend(
        1, places, after(bounds, first_grads), near_grads, far_grads, second_recv, (ids,)
    )
    second_out = swap(second_grads)

    across = packs // depth
    order = jnp.stack([(position // depth + step) % across for step in range(across)]).astype(jnp.int32)
    contexts = (first_context, second_context)
    parts = after(project(D // packs, depth, order, contexts, near + far), first_out)
    others = []
    for step in range(1, across):
        pairs = [(j, (j + step * depth) % packs) for j in range(packs)]
        others.append(lax.ppermute(parts[step], "dp", pairs))

    total = parts[0].astype(F32) + sum(other.astype(F32) for other in others)
    rows = [[x * depth + z for z in range(depth)] for x in range(across)]
    parts = lax.all_to_all(
        after(total.astype(BF16), second_out), "dp", split_axis=0, concat_axis=0, axis_index_groups=rows
    )
    projection_grad = unfolded(jnp.sum(parts.astype(F32), axis=0)).T

    query_grad, key_grad, value_grad = unpack(first_out, second_out)
    return (query_grad, key_grad, value_grad, projection_grad)


def solution(mesh):
    return jax.shard_map(
        shards,
        mesh=mesh,
        in_specs=(
            P("dp", "seq", None),
            P("dp", "seq", None),
            P("dp", "seq", None),
            P("dp", "seq", None),
            P(None, "dp"),
            P("dp", "seq"),
        ),
        out_specs=(
            P("dp", "seq", None),
            P("dp", "seq", None),
            P("dp", "seq", None),
            P("seq", "dp"),
        ),
        check_vma=False,
    )
```

```python
import functools
import math

import jax
import jax.numpy as jnp
from jax import lax
from jax.experimental import pallas as pl
from jax.experimental.pallas import tpu as pltpu
from jax.sharding import PartitionSpec as P

D = 1536
HEADS = 16
HEAD = D // HEADS
SEQ = 8
OWN = HEADS // SEQ
WIDTH = OWN * HEAD
ROWS = 256
IDS = 16
SCALING = 1.0 / math.sqrt(HEAD)
LOG2E = math.log2(math.e)
EXCLUDED = -1e30
VMEM_BYTES = 20 * 1024 * 1024
ATTENTION_VMEM_BYTES = 56 * 1024 * 1024

BF16 = jnp.bfloat16
F32 = jnp.float32


def whole(count):
    return [pl.BlockSpec(memory_space=pltpu.VMEM)] * count


def dot(left, right, left_dim=1, right_dim=0):
    return lax.dot_general(
        left, right, (((left_dim,), (right_dim,)), ((), ())), preferred_element_type=F32
    )


def pack_kernel(query_ref, key_ref, value_ref, ids_ref, *outs):
    for number, ref in enumerate((query_ref, key_ref, value_ref)):
        at = slice(number * HEAD, (number + 1) * HEAD)
        for group in range(SEQ // 2):
            width = 2 * WIDTH
            turned = ref[0, :, group * width : (group + 1) * width].T
            for part in range(2 * OWN):
                outs[part % OWN][2 * group + part // OWN, at, :] = turned[
                    part * HEAD : (part + 1) * HEAD
                ]
    ids = jnp.broadcast_to(ids_ref[...].astype(F32), (IDS, ROWS)).astype(BF16)
    for block in range(SEQ):
        outs[0][block, 3 * HEAD :, :] = ids


def pack(queries, keys, values, utterance):
    return pl.pallas_call(
        pack_kernel,
        out_shape=tuple(
            jax.ShapeDtypeStruct((SEQ, 3 * HEAD + (IDS if head == 0 else 0), ROWS), BF16)
            for head in range(OWN)
        ),
        in_specs=whole(4),
        out_specs=tuple(whole(OWN)),
        compiler_params=pltpu.CompilerParams(vmem_limit_bytes=VMEM_BYTES),
        cost_estimate=pl.CostEstimate(flops=2 * 10**10, bytes_accessed=5 * 10**6, transcendentals=0),
        name="pack",
    )(queries, keys, values, utterance)


def unpack_kernel(first_ref, second_ref, query_ref, key_ref, value_ref):
    for number, ref in enumerate((query_ref, key_ref, value_ref)):
        at = slice(number * HEAD, (number + 1) * HEAD)
        for group in range(SEQ // 2):
            parts = [
                part[block, at, :]
                for block in (2 * group, 2 * group + 1)
                for part in (first_ref, second_ref)
            ]
            width = 2 * WIDTH
            ref[0, :, group * width : (group + 1) * width] = jnp.concatenate(parts, axis=0).T


def unpack(first, second):
    steps = 2
    rows = ROWS // steps
    shape = jax.ShapeDtypeStruct((1, ROWS, D), BF16)
    part = pl.BlockSpec((SEQ, 3 * HEAD, rows), lambda step: (0, 0, step))
    whole_rows = pl.BlockSpec((1, rows, D), lambda step: (0, step, 0))
    return pl.pallas_call(
        unpack_kernel,
        grid=(steps,),
        out_shape=(shape, shape, shape),
        in_specs=[part, part],
        out_specs=(whole_rows,) * 3,
        compiler_params=pltpu.CompilerParams(vmem_limit_bytes=VMEM_BYTES),
        cost_estimate=pl.CostEstimate(flops=10**7, bytes_accessed=5 * 10**6, transcendentals=0),
        name="unpack",
    )(first, second)


def fold(tile, op):
    return op(tile.reshape(tile.shape[0] // 8, 8, tile.shape[1]), axis=0)


def rows_of(block):
    return pl.ds(pl.multiple_of(block * ROWS, ROWS), ROWS)


NEAR = ((0, 256),) * 6
FAR = ((0, 128), (128, 128)) * 2


def gradient_kernel(rows, weight_ref, *refs):
    pieces, out_ref = refs[: len(rows)], refs[len(rows)]
    for number, (piece, (first, count)) in enumerate(zip(pieces, rows, strict=True)):
        local = sum(size for _, size in rows[:number]) // ROWS
        out_ref[local, :, first : first + count] = (
            dot(piece[...], weight_ref[...]).astype(BF16).T
        )


def gradients(weight, pieces, rows):
    blocks = sum(size for _, size in rows) // ROWS
    return pl.pallas_call(
        functools.partial(gradient_kernel, rows),
        out_shape=jax.ShapeDtypeStruct((blocks, WIDTH, ROWS), BF16),
        in_specs=whole(1 + len(rows)),
        out_specs=pl.BlockSpec(memory_space=pltpu.VMEM),
        compiler_params=pltpu.CompilerParams(vmem_limit_bytes=VMEM_BYTES),
        cost_estimate=pl.CostEstimate(
            flops=blocks * 16 * 10**7, bytes_accessed=blocks * 10**6, transcendentals=0
        ),
        name="gradients",
    )(weight, *pieces)


FIXED = 5
UNROLL = 4


def over(low, high, body, carry):
    if isinstance(high, list):
        return body(high, carry)
    chunk = UNROLL
    while chunk:
        steps = (high - low) // chunk
        carry = lax.fori_loop(
            0,
            steps,
            lambda step, held, low=low, chunk=chunk: body(
                [low + step * chunk + i for i in range(chunk)], held
            ),
            carry,
        )
        low = low + steps * chunk
        chunk //= 2
    return carry


def slot_of(block, high):
    return [other is block for other in high].index(True) if isinstance(high, list) else block


def each_block(place_ref, low_ref, high_ref, query_block):
    def any_block(place, _):
        index = place_ref[place]
        low, high = low_ref[index], high_ref[index]
        for count in range(1, FIXED + 1):

            @pl.when(high - low == count)
            def _(count=count):
                query_block(place, low, [low + i for i in range(count)])

        @pl.when(high - low > FIXED)
        def _():
            query_block(place, low, high)

        return 0

    lax.fori_loop(0, SEQ, any_block, 0)


def attend_kernel(head, place_ref, low_ref, high_ref, near_ref, far_ref, recv_ref, *refs):
    if head == 0:
        out_ref, context_ref, ids_ref, *refs = refs
    else:
        ids_ref, out_ref, context_ref, *refs = refs
    grads, kid_ref, key_nat, value_nat, score_ref, key_acc, value_acc = refs
    at = slice(head * HEAD, (head + 1) * HEAD)
    query_at, key_at, value_at = (slice(i * HEAD, (i + 1) * HEAD) for i in range(3))
    for block in range(SEQ):
        rows = slice(block * ROWS, (block + 1) * ROWS)
        key_nat[rows, :] = recv_ref[block, key_at, :].T
        value_nat[rows, :] = recv_ref[block, value_at, :].T
        if head == 0:
            ids_ref[block] = recv_ref[block, 3 * HEAD :, :].astype(F32)[:8]
        kid_ref[rows, :] = jnp.broadcast_to(ids_ref[block, 0:1, :], (128, ROWS)).T
    grads[: len(NEAR)] = near_ref[:, at, :]
    grads[len(NEAR) :] = far_ref[:, at, :]
    key_acc[...] = jnp.zeros_like(key_acc)
    value_acc[...] = jnp.zeros_like(value_acc)

    def query_block(place, low, high):
        index = place_ref[place]
        queries = recv_ref[index, query_at, :]
        block_grads = grads[place]
        query_id = ids_ref[index, 0:1, :]

        def first(blocks, top):
            for block in blocks:
                key_id = kid_ref[rows_of(block), :]
                keep = jnp.concatenate([key_id, key_id], axis=1) == query_id
                scores = jnp.where(keep, dot(key_nat[rows_of(block), :], queries), EXCLUDED)
                score_ref[slot_of(block, high)] = scores
                top = jnp.maximum(top, fold(scores, jnp.max))
            return top

        top = over(low, high, first, jnp.full((8, ROWS), EXCLUDED, F32))
        top = jnp.max(top, axis=0, keepdims=True) * (SCALING * LOG2E)

        def second(blocks, carry):
            total, context = carry
            for block in blocks:
                shifted = jnp.exp2(score_ref[slot_of(block, high)] * (SCALING * LOG2E) - top)
                score_ref[slot_of(block, high)] = shifted
                total = total + fold(shifted, jnp.sum)
                context = context + dot(recv_ref[block, value_at, :], shifted.astype(BF16))
            return total, context

        total, context = over(
            low, high, second, (jnp.zeros((8, ROWS), F32), jnp.zeros((HEAD, ROWS), F32))
        )
        inverse = 1.0 / jnp.sum(total, axis=0, keepdims=True)
        context = (context * inverse).astype(BF16)
        context_ref[place] = context
        row_terms = jnp.sum(block_grads.astype(F32) * context.astype(F32), axis=0, keepdims=True)

        def third(blocks, query_total):
            added = []
            for block in blocks:
                rows = rows_of(block)
                weights = score_ref[slot_of(block, high)] * inverse
                weights_grad = dot(value_nat[rows, :], block_grads)
                score_grad = (weights * (weights_grad - row_terms)).astype(BF16)
                value_part = dot(weights.astype(BF16), block_grads, 1, 1)
                key_part = dot(score_grad, queries, 1, 1)
                query_total = query_total + dot(recv_ref[block, key_at, :], score_grad)
                added.append((rows, value_part, key_part))
            for rows, value_part, key_part in added:
                value_acc[rows, :] += value_part
                key_acc[rows, :] += key_part
            return query_total

        query_total = over(low, high, third, jnp.zeros((HEAD, ROWS), F32))
        out_ref[index, query_at, :] = (query_total * SCALING).astype(BF16)

    each_block(place_ref, low_ref, high_ref, query_block)
    for block in range(SEQ):
        rows = slice(block * ROWS, (block + 1) * ROWS)
        out_ref[block, key_at, :] = (key_acc[rows, :] * SCALING).astype(BF16).T
        out_ref[block, value_at, :] = value_acc[rows, :].astype(BF16).T


def attend(head, places, bounds, near, far, recv, ids=()):
    shapes = [
        jax.ShapeDtypeStruct((SEQ, 3 * HEAD, ROWS), BF16),
        jax.ShapeDtypeStruct((SEQ, HEAD, ROWS), BF16),
    ]
    if head == 0:
        shapes.append(jax.ShapeDtypeStruct((SEQ, 8, ROWS), F32))
    return pl.pallas_call(
        functools.partial(attend_kernel, head),
        out_shape=tuple(shapes),
        in_specs=[pl.BlockSpec(memory_space=pltpu.SMEM)] * 3 + whole(3 + len(ids)),
        out_specs=tuple(whole(len(shapes))),
        scratch_shapes=[
            pltpu.VMEM((SEQ, HEAD, ROWS), BF16),
            pltpu.VMEM((SEQ * ROWS, 128), F32),
            pltpu.VMEM((SEQ * ROWS, HEAD), BF16),
            pltpu.VMEM((SEQ * ROWS, HEAD), BF16),
            pltpu.VMEM((SEQ, ROWS, ROWS), F32),
            pltpu.VMEM((SEQ * ROWS, HEAD), F32),
            pltpu.VMEM((SEQ * ROWS, HEAD), F32),
        ],
        compiler_params=pltpu.CompilerParams(vmem_limit_bytes=ATTENTION_VMEM_BYTES),
        cost_estimate=pl.CostEstimate(
            flops=2 * 10**10, bytes_accessed=6 * 10**6, transcendentals=4 * 10**6
        ),
        name="attend",
    )(places, *bounds, near, far, recv, *ids)


def folded(part):
    half = part.shape[0] // 2
    return jnp.concatenate(
        [part[:, :128], jnp.concatenate([part[:half, 128:], part[half:, 128:]], axis=1)], axis=0
    )


def unfolded(part):
    columns = part.shape[0] * 2 // 3
    right = jnp.concatenate([part[columns:, :64], part[columns:, 64:]], axis=0)
    return jnp.concatenate([part[:columns], right], axis=1)


def project_kernel(columns, depth, x_ref, *refs):
    rows = NEAR + FAR
    contexts, refs = refs[:OWN], refs[OWN:]
    pieces, outs, (total_ref, turned_ref) = refs[: len(rows)], refs[len(rows) : -2], refs[-2:]
    for number, (piece, (first, count)) in enumerate(zip(pieces, rows, strict=True)):
        local = sum(size for _, size in rows[:number]) // ROWS
        context = jnp.concatenate([ref[local, :, first : first + count] for ref in contexts], axis=0)
        part = dot(context, piece[...])
        if number == 0:
            total_ref[...] = part
        else:
            total_ref[...] += part
    turned_ref[...] = total_ref[...].T
    for step, out_ref in enumerate(outs):
        for z in range(depth):
            start = pl.multiple_of((x_ref[step] * depth + z) * columns, 16)
            out_ref[z] = folded(turned_ref[pl.ds(start, columns), :]).astype(BF16)


def project(columns, depth, order, contexts, pieces):
    across = order.shape[0]
    return pl.pallas_call(
        functools.partial(project_kernel, columns, depth),
        out_shape=(jax.ShapeDtypeStruct((depth, columns * 3 // 2, 128), BF16),) * across,
        in_specs=[pl.BlockSpec(memory_space=pltpu.SMEM)] + whole(OWN + len(pieces)),
        out_specs=tuple(whole(across)),
        scratch_shapes=[pltpu.VMEM((WIDTH, D), F32), pltpu.VMEM((D, WIDTH), F32)],
        compiler_params=pltpu.CompilerParams(vmem_limit_bytes=VMEM_BYTES),
        cost_estimate=pl.CostEstimate(
            flops=12 * 10**8, bytes_accessed=7 * 10**6, transcendentals=0
        ),
        name="project",
    )(order, *contexts, *pieces)


PLACES = ((0, 0), (0, 1), (3, 0), (3, 1), (1, 0), (1, 1), (2, 0), (2, 1))


def moved(j, step, other):
    return ((j // 2 + step) % 4) * 2 + (j % 2 ^ other)


def after(arrays, *others):
    return lax.optimization_barrier((arrays, others))[0]


def shards(queries, keys, values, out_grad, out_weight, utterance):
    packs = lax.axis_size("dp")
    depth = math.gcd(packs, 8)
    me, position = lax.axis_index("seq"), lax.axis_index("dp")
    grads = out_grad[0]
    places = jnp.stack([moved(me, *place) for place in PLACES]).astype(jnp.int32)

    def send(array, step, other):
        return lax.ppermute(array, "seq", [(j, moved(j, step, other)) for j in range(SEQ)])

    def swap(array):
        return lax.all_to_all(array, "seq", split_axis=0, concat_axis=0)

    up, down = send(grads, 1, 0), send(grads, 3, 0)
    swapped = send(grads, 0, 1)
    far_up, far_down = send(up[:128], 1, 0), send(down[128:], 3, 0)
    near = (grads, swapped, up, send(up, 0, 1), down, send(down, 0, 1))

    packed = pack(queries, keys, values, utterance)
    own_rows = lax.dynamic_slice_in_dim(out_weight, me * WIDTH, WIDTH, 0).T
    own_rows = folded(own_rows)
    own_rows = jnp.broadcast_to(own_rows[None], (packs,) + own_rows.shape)
    folded_weight = lax.all_to_all(own_rows, "dp", split_axis=0, concat_axis=0)
    weight = jax.vmap(unfolded)(folded_weight).reshape(D, WIDTH)

    first_recv = swap(after(packed[0], folded_weight, far_up, far_down))
    second_recv = swap(after(packed[1], first_recv))
    near_grads = gradients(weight, near, NEAR)
    far_up, far_down = after((far_up, far_down), near_grads)
    far = (far_up, far_down, send(far_up, 0, 1), send(far_down, 0, 1))
    far_grads = gradients(weight, far, FAR)

    starts, ends = (first_recv[:, 3 * HEAD, at].astype(jnp.int32) for at in (0, ROWS - 1))
    bounds = (
        jnp.sum((ends[None, :] < starts[:, None]).astype(jnp.int32), axis=1),
        jnp.sum((starts[None, :] <= ends[:, None]).astype(jnp.int32), axis=1),
    )

    first_grads, first_context, ids = attend(
        0, places, bounds, near_grads, far_grads, first_recv
    )
    first_out = swap(after(first_grads, second_recv))
    second_grads, second_context = attend(
        1, places, after(bounds, first_grads), near_grads, far_grads, second_recv, (ids,)
    )
    second_out = swap(second_grads)

    across = packs // depth
    order = jnp.stack([(position // depth + step) % across for step in range(across)]).astype(jnp.int32)
    contexts = (first_context, second_context)
    parts = after(project(D // packs, depth, order, contexts, near + far), first_out)
    others = []
    for step in range(1, across):
        pairs = [(j, (j + step * depth) % packs) for j in range(packs)]
        others.append(lax.ppermute(parts[step], "dp", pairs))

    total = parts[0].astype(F32) + sum(other.astype(F32) for other in others)
    rows = [[x * depth + z for z in range(depth)] for x in range(across)]
    parts = lax.all_to_all(
        after(total.astype(BF16), second_out), "dp", split_axis=0, concat_axis=0, axis_index_groups=rows
    )
    projection_grad = unfolded(jnp.sum(parts.astype(F32), axis=0)).T

    query_grad, key_grad, value_grad = unpack(first_out, second_out)
    return (query_grad, key_grad, value_grad, projection_grad)


def solution(mesh):
    return jax.shard_map(
        shards,
        mesh=mesh,
        in_specs=(
            P("dp", "seq", None),
            P("dp", "seq", None),
            P("dp", "seq", None),
            P("dp", "seq", None),
            P(None, "dp"),
            P("dp", "seq"),
        ),
        out_specs=(
            P("dp", "seq", None),
            P("dp", "seq", None),
            P("dp", "seq", None),
            P("seq", "dp"),
        ),
        check_vma=False,
    )
```
